32 devices in a mesh: ctx: 4 (over x, core), head: 8 (over z, y).
Axes of the slice: x: 2, y: 2, z: 4, core: 2. Of those that a mesh axis runs over, the one named last changes fastest.
Arguments:
- q_nope: bfloat16 [512, 32, 128], P('ctx', 'head'), may hold values from -6 to 6
- q_rope: bfloat16 [512, 32, 64], P('ctx', 'head'), may hold values from -300 to 300
- w_uk: bfloat16 [32, 128, 512], P('head'), may hold values from -0.5 to 0.5
- w_uv: bfloat16 [32, 512, 128], P('head'), may hold values from -0.75 to 0.75
- w_o: bfloat16 [4096, 7168], P('head', 'ctx'), may hold values from -0.25 to 0.25
- cache_kv: bfloat16 [512, 576], P('ctx'), may hold values from -4 to 4
- new_kv: bfloat16 [512, 576], P('ctx'), may hold values from -4 to 4
- block_order: int32 [4], replicated, may hold values from 0 to 3, each once
- cache_lengths: int32 [4], replicated, may hold values from 32 to 128, as said below
Outputs:
- mixed: bfloat16 [512, 7168], P(('ctx', 'head'))
The draws below stay inside these ranges and needn't reach their ends.
Inputs may be any that keep to these rules, and one draw needn't show every extreme that they name: `cache_lengths`: at least one ctx index has all 128 slots valid.
All inputs are finite; a program needn't handle non-finite values.
Results may differ from the reference program's by a relative error of at most 0.024.
Values may be sent and summed in bfloat16 or wider, within the bound.
A program may use at most 64 MiB of HBM per device.

```python
import jax
import jax.numpy as jnp
from jax import lax

D = 7168
LATENT = 512
ROPE = 64
NOPE = 128
VDIM = 128
TQ_DEV = 128
SK_DEV = 128
HEADS = 32
TOKENS = 512
CACHE = 512
N_CTX = 4


def base_cache(key):
    values = jax.random.normal(jax.random.fold_in(key, 11), (CACHE, LATENT + ROPE), jnp.float32)
    return jnp.clip(values, -4.0, 4.0)


def draw_cache_kv(key, part):
    values = base_cache(key)
    return values.astype(jnp.bfloat16)


def draw_q_rope(key, part):
    values = jax.random.normal(jax.random.fold_in(key, 23), (TOKENS, HEADS, ROPE), jnp.float32)
    values = jnp.clip(values, -4.0, 4.0)
    return values.astype(jnp.bfloat16)


def draw_cache_lengths(key, part):
    shard_count = CACHE // SK_DEV
    values = jax.random.randint(jax.random.fold_in(key, 5), (shard_count,), SK_DEV // 4, SK_DEV + 1)
    fullest = jax.random.randint(jax.random.fold_in(key, 7), (), 0, shard_count)
    return jnp.where(jnp.arange(shard_count) == fullest, SK_DEV, values).astype(jnp.int32)


def levels(own_key, dims, cuts, smallest, top_value):
    def one(axis_at, parts):
        draws = jax.random.uniform(jax.random.fold_in(jax.random.fold_in(own_key, 6), axis_at), (parts,), jnp.float32, smallest / len(cuts), top_value / len(cuts))
        return jnp.repeat(jnp.exp(draws), dims[axis_at] // parts).reshape((-1,) + (1,) * (len(dims) - axis_at - 1))

    level = one(*cuts[0])
    for cut in cuts[1:]:
        level = level * one(*cut)
    return level


def bell_draw(rng, shape, width, limit, pieces=(), kind=jnp.bfloat16):
    drawn = width * jax.random.normal(rng, shape, jnp.float32)
    if pieces:
        drawn = drawn * levels(rng, shape, pieces, -0.22, 0.18)
    return jnp.clip(drawn, -limit, limit).astype(kind)


def setup_inputs(seed: int = 0) -> dict:
    seeds = jax.random.split(jax.random.key(seed), 10)
    return {
        "q_nope": bell_draw(seeds[0], (TOKENS, HEADS, NOPE), 1.5, 6.0, ((0, 4), (1, 8))),
        "q_rope": draw_q_rope(jax.random.fold_in(seeds[9], 71), 0),
        "w_uk": bell_draw(seeds[2], (HEADS, NOPE, LATENT), NOPE ** -0.5, 0.5, ((0, 8),)),
        "w_uv": bell_draw(seeds[3], (HEADS, LATENT, VDIM), (LATENT // 8) ** -0.5, 0.75, ((0, 8),)),
        "w_o": bell_draw(seeds[4], (HEADS * VDIM, D), (HEADS * VDIM // 8) ** -0.5, 0.25, ((0, 8), (1, 4))),
        "cache_kv": draw_cache_kv(jax.random.fold_in(seeds[9], 71), 0),
        "new_kv": bell_draw(seeds[6], (TOKENS, LATENT + ROPE), 1.0, 4.0, ((0, 4),)),
        "block_order": jax.random.permutation(seeds[7], N_CTX).astype(jnp.int32),
        "cache_lengths": draw_cache_lengths(jax.random.fold_in(seeds[9], 71), 0),
    }


neg_large = -1.0e30


def reference(q_nope, q_rope, w_uk, w_uv, w_o, cache_kv, new_kv, block_order, cache_lengths):
    score_scale = float(NOPE + ROPE) ** -0.5
    token_ids = jnp.arange(TOKENS, dtype=jnp.int32)
    query_pos = block_order[token_ids // TQ_DEV] * TQ_DEV + token_ids % TQ_DEV
    slot_ids = jnp.arange(CACHE, dtype=jnp.int32)
    cache_valid = (slot_ids % SK_DEV) < cache_lengths[slot_ids // SK_DEV]
    visible = jnp.concatenate(
        [jnp.broadcast_to(cache_valid[None, :], (TOKENS, CACHE)), query_pos[None, :] <= query_pos[:, None]], axis=1)
    all_keys = jnp.concatenate([cache_kv, new_kv], axis=0)
    key_latent = all_keys[:, :LATENT]

    def one_head(inputs):
        nope_part, rope_part, up_key, up_value = inputs
        latent_query = jnp.dot(nope_part, up_key, preferred_element_type=jnp.float32)
        query = jnp.concatenate([latent_query, rope_part.astype(jnp.float32)], axis=1).astype(jnp.bfloat16)
        scores = lax.dot_general(query, all_keys, (((1,), (1,)), ((), ())),
                                 preferred_element_type=jnp.float32) * score_scale
        highest = jnp.max(jnp.where(visible, scores, neg_large), axis=1)
        expo = jnp.where(visible, jnp.exp(scores - highest[:, None]), 0.0)
        totals = jnp.sum(expo, axis=1)
        weighted = jnp.dot(expo.astype(jnp.bfloat16), key_latent, preferred_element_type=jnp.float32)
        latent_out = (weighted / totals[:, None]).astype(jnp.bfloat16)
        return jnp.dot(latent_out, up_value, preferred_element_type=jnp.float32).astype(jnp.bfloat16)

    head_out = lax.map(one_head, (jnp.transpose(q_nope, (1, 0, 2)), jnp.transpose(q_rope, (1, 0, 2)), w_uk, w_uv))
    flat_out = jnp.transpose(head_out, (1, 0, 2)).reshape(TOKENS, HEADS * VDIM)
    return jnp.dot(flat_out, w_o, preferred_element_type=jnp.float32).astype(jnp.bfloat16)
```

```python
import functools

import jax
import jax.numpy as jnp
from jax import lax
from jax.experimental import pallas as pl
from jax.experimental.pallas import tpu as pltpu
from jax.sharding import PartitionSpec as P

neg_large = -1e30
MESH = pl.DeviceIdType.MESH


def plain_on_device(q_nope, q_rope, w_uk, w_uv, w_o, cache_kv, new_kv, block_order, cache_lengths):
    tok_rows, heads_here, nope_width = q_nope.shape
    latent_width = w_uk.shape[2]
    value_width = w_uv.shape[2]
    cache_rows = cache_kv.shape[0]
    shard_rows = cache_rows + tok_rows
    ctx_count = lax.axis_size("ctx")
    head_count = lax.axis_size("head")
    score_scale = float(nope_width + q_rope.shape[2]) ** (-0.5)
    query_rows = tok_rows * heads_here
    q_latent = jnp.einsum("thn,hnc->thc", q_nope, w_uk, preferred_element_type=jnp.float32)
    query = jnp.concatenate([q_latent, q_rope.astype(jnp.float32)], axis=2).astype(jnp.bfloat16)
    query = query.reshape(query_rows, query.shape[2])
    shard_ids = jnp.arange(ctx_count, dtype=jnp.int32)
    own_block = jnp.sum(jnp.where(shard_ids == lax.axis_index("ctx"), block_order, 0))
    query_pos = own_block * tok_rows + jnp.arange(query_rows, dtype=jnp.int32) // heads_here
    local_keys = jnp.concatenate([cache_kv, new_kv], axis=0)
    piece = lax.all_gather(local_keys, "ctx", axis=0, tiled=True)
    global_rows = jnp.arange(piece.shape[0], dtype=jnp.int32)
    owners = global_rows // shard_rows
    offsets = global_rows % shard_rows
    matches = owners[:, None] == shard_ids[None, :]
    lengths = jnp.sum(jnp.where(matches, cache_lengths[None, :], 0), axis=1)
    blocks = jnp.sum(jnp.where(matches, block_order[None, :], 0), axis=1)
    key_pos = blocks * tok_rows + offsets - cache_rows
    visible = jnp.where(
        (offsets < cache_rows)[None, :],
        (offsets < lengths)[None, :],
        key_pos[None, :] <= query_pos[:, None],
    )
    best = jnp.full((query_rows,), neg_large, jnp.float32)
    scores = (
        lax.dot_general(query, piece, (((1,), (1,)), ((), ())), preferred_element_type=jnp.float32)
        * score_scale
    )
    fresh = jnp.maximum(best, jnp.max(jnp.where(visible, scores, neg_large), axis=1))
    expo = jnp.where(visible, jnp.exp(scores - fresh[:, None]), 0.0)
    totals = jnp.sum(expo, axis=1)
    accum = jnp.dot(
        expo.astype(jnp.bfloat16), piece[:, :latent_width], preferred_element_type=jnp.float32
    )
    best, totals, accum = (fresh, totals, accum)
    latent_out = (
        (accum / totals[:, None]).astype(jnp.bfloat16).reshape(tok_rows, heads_here, latent_width)
    )
    head_out = jnp.einsum("thc,hcv->thv", latent_out, w_uv, preferred_element_type=jnp.float32)
    head_out = head_out.astype(jnp.bfloat16).reshape(tok_rows, heads_here * value_width)
    partial_rows = jnp.dot(
        lax.all_gather(head_out, "ctx", axis=0, tiled=True), w_o, preferred_element_type=jnp.float32
    )
    column_width = w_o.shape[1]
    own_rows = tok_rows // head_count
    grouped = partial_rows.reshape(ctx_count, head_count, own_rows, column_width)
    summed = lax.psum_scatter(grouped.astype(jnp.bfloat16), "head", scatter_dimension=1, tiled=True)
    regrouped = lax.all_to_all(summed, "ctx", split_axis=0, concat_axis=3, tiled=True)
    return regrouped.reshape(own_rows, ctx_count * column_width)


def flip(index, bit):
    return index + bit - 2 * bit * lax.rem(lax.div(index, bit), 2)


def flip_all(index, mask):
    bit = 1
    while bit <= mask:
        if mask & bit:
            index = flip(index, bit)
        bit *= 2
    return index


def bits_of(count):
    return [1 << k for k in range(count.bit_length() - 1)]


def low_bit(mask):
    return mask & -mask


def column_groups(width, head_bits):
    if len(head_bits) < 2:
        return [(0, width, tuple(head_bits))]
    first = (width * 5 // 7) // 128 * 128
    swapped = (head_bits[1], head_bits[0]) + tuple(head_bits[2:])
    return [(0, first, tuple(head_bits)), (first, width - first, swapped)]


def kernel(dims, qn_ref, qr_ref, uk_ref, uv_hbm, wo_hbm, ck_ref, nk_ref, order_ref, lens_ref, out_ref, *scratch):
    n_ctx, n_head, tok, heads, nope, rope, latent, vdim, slots, groups = dims
    n_groups = len(groups)
    query, kv, acc, ho, uv_ref, wo_ref = scratch[:6]
    snd = scratch[6 : 6 + n_groups]
    rcv = scratch[6 + n_groups : 6 + 2 * n_groups]
    tot = scratch[6 + 2 * n_groups : 6 + 3 * n_groups]
    loc_sem, kv_ssem, kv_rsem, ho_ssem, ho_rsem, rs_ssem, rs_rsem, out_ssem, out_rsem = scratch[6 + 3 * n_groups :]
    ctx, hd = lax.axis_index("ctx"), lax.axis_index("head")
    ctx_bits, head_bits = bits_of(n_ctx), bits_of(n_head)
    nb = len(head_bits)
    own = tok // n_head
    keys = slots + tok
    rows = heads * tok
    f32, bf16 = jnp.float32, jnp.bfloat16

    def peer(ctx_mask=0, head_bit=0):
        return {
            "ctx": flip_all(ctx, ctx_mask),
            "head": flip(hd, head_bit) if head_bit else hd,
        }

    local = [
        pltpu.make_async_copy(ck_ref, kv.at[0, :, 0:slots], loc_sem.at[0]),
        pltpu.make_async_copy(nk_ref, kv.at[0, :, slots:keys], loc_sem.at[1]),
        pltpu.make_async_copy(uv_hbm, uv_ref, loc_sem.at[2]),
        pltpu.make_async_copy(wo_hbm, wo_ref, loc_sem.at[3]),
    ]
    for copy in local:
        copy.start()

    barrier = pltpu.get_barrier_semaphore()
    for mask in range(1, n_ctx):
        pl.semaphore_signal(barrier, inc=1, device_id=peer(mask), device_id_type=MESH)
    for bit in head_bits:
        pl.semaphore_signal(barrier, inc=1, device_id=peer(0, bit), device_id_type=MESH)
    pl.semaphore_wait(barrier, n_ctx - 1 + nb)

    sends = []

    def send(src, dst, ssem, rsem, device):
        copy = pltpu.make_async_remote_copy(
            src_ref=src, dst_ref=dst, send_sem=ssem, recv_sem=rsem, device_id=device, device_id_type=MESH
        )
        copy.start()
        sends.append(copy)
        return copy

    kv_in = {}
    spans = [(0, slots), (slots, keys)]

    def pass_keys(mask, part):
        lo, hi = spans[part]
        for bit in reversed(ctx_bits):
            if mask == 0 or bit < low_bit(mask):
                src = (ck_ref, nk_ref)[part] if mask == 0 else kv.at[mask, :, lo:hi]
                kv_in[mask | bit, part] = send(
                    src,
                    kv.at[mask | bit, :, lo:hi],
                    kv_ssem.at[mask | bit, part],
                    kv_rsem.at[mask | bit, part],
                    peer(bit),
                )

    for part in range(2):
        pass_keys(0, part)

    order0 = groups[0][2]
    place = lax.broadcasted_iota(jnp.int32, (tok, 1), 0)
    block = place // own
    token = place % own
    for at, bit in enumerate(order0):
        digit = (block // (1 << (nb - 1 - at))) % 2
        mine = lax.rem(lax.div(hd, bit), 2)
        token = token + own * bit * (digit + mine - 2 * digit * mine)
    flat = lax.broadcasted_iota(jnp.int32, (tok, rows), 1)
    pick = (lax.broadcasted_iota(jnp.int32, (tok, tok), 1) == token).astype(bf16)
    q_all = qn_ref[...]
    for h in range(heads):
        choose = (flat == token * heads + h).astype(bf16)
        q_h = jnp.dot(choose, q_all, preferred_element_type=f32).astype(bf16)
        lat = jnp.dot(q_h, uk_ref[h], preferred_element_type=f32)
        span = slice(h * tok, (h + 1) * tok)
        query[span, 0:latent] = lat.astype(bf16)
        turned = lax.dot_general(pick, qr_ref[h], (((1,), (1,)), ((), ())), preferred_element_type=f32)
        query[span, latent : latent + rope] = turned.astype(bf16)

    scale = float(nope + rope) ** (-0.5)
    q_pos = order_ref[ctx] * tok + jnp.concatenate([token] * heads, axis=0)
    col = lax.broadcasted_iota(jnp.int32, (rows, keys), 1)

    best = total = None
    for mask in range(n_ctx):
        for part in range(2):
            if mask == 0:
                local[part].wait()
            else:
                kv_in[mask, part].wait_recv()
                pass_keys(mask, part)
        source = flip_all(ctx, mask)
        length = lens_ref[source]
        key_pos = col - slots + order_ref[source] * tok
        seen = jnp.where(col < slots, col - length + 1, key_pos - q_pos) <= 0
        s = jnp.dot(query[...], kv[mask], preferred_element_type=f32) * scale
        s = jnp.where(seen, s, neg_large)
        top = jnp.max(s, axis=1, keepdims=True)
        if mask:
            top = jnp.maximum(best, top)
        e = jnp.exp(s - top)
        part_sum = jnp.sum(e, axis=1, keepdims=True)
        mixed = lax.dot_general(
            e.astype(bf16), kv[mask, 0:latent, :], (((1,), (1,)), ((), ())), preferred_element_type=f32
        )
        if mask:
            shrink = jnp.exp(best - top)
            total = total * shrink + part_sum
            mixed = acc[...] * shrink + mixed
        else:
            total = part_sum
        best = top
        if mask < n_ctx - 1:
            acc[...] = mixed

    lat_out = (mixed / total).astype(bf16)
    local[2].wait()
    for h in range(heads):
        ho[0, :, h * vdim : (h + 1) * vdim] = jnp.dot(
            lat_out[h * tok : (h + 1) * tok], uv_ref[h], preferred_element_type=f32
        ).astype(bf16)
    ho_in = {}

    def pass_heads(mask):
        for bit in reversed(ctx_bits):
            if mask == 0 or bit < low_bit(mask):
                ho_in[mask | bit] = send(
                    ho.at[mask], ho.at[mask | bit], ho_ssem.at[mask | bit], ho_rsem.at[mask | bit], peer(bit)
                )

    pass_heads(0)
    local[3].wait()

    items = [(mask, g) for mask in range(n_ctx) for g in range(n_groups)]
    moving = {}

    def push(at, step):
        mask, g = items[at]
        size = tok >> (step + 1)
        moving[at, step] = send(
            snd[g].at[mask, size : 2 * size],
            rcv[g].at[mask, size : 2 * size],
            rs_ssem.at[at, step],
            rs_rsem.at[at, step],
            peer(0, groups[g][2][step]),
        )

    def first_step(at):
        mask, g = items[at]
        lo, width, order = groups[g]
        x = ho[mask]
        if order != order0:
            def at_block(p):
                m = sum(order[k] for k in range(nb) if p >> (nb - 1 - k) & 1)
                return sum(1 << (nb - 1 - k) for k in range(nb) if m & order0[k])

            x = jnp.concatenate([x[at_block(p) * own : (at_block(p) + 1) * own] for p in range(n_head)], axis=0)
        y = jnp.dot(x, wo_ref[:, lo : lo + width], preferred_element_type=f32)
        tot[g][mask] = y[0 : tok // 2]
        snd[g][mask, tok // 2 : tok] = y[tok // 2 :].astype(bf16)
        push(at, 0)

    def later_step(at, step):
        mask, g = items[at]
        lo, width, order = groups[g]
        size = tok >> step
        moving[at, step - 1].wait_recv()
        y = tot[g][mask, 0:size] + rcv[g][mask, size : 2 * size].astype(f32)
        if step < nb:
            half = size // 2
            snd[g][mask, half:size] = y[half:].astype(bf16)
            tot[g][mask, 0:half] = y[:half]
            push(at, step)
        elif mask == 0:
            out_ref[ctx, :, lo : lo + width] = y.astype(bf16)
        else:
            snd[g][mask, 0:own] = y.astype(bf16)
            send(
                snd[g].at[mask, 0:own],
                out_ref.at[ctx, :, lo : lo + width],
                out_ssem.at[at],
                out_rsem.at[at],
                peer(mask),
            )

    for at, (mask, g) in enumerate(items):
        if mask and g == 0:
            ho_in[mask].wait_recv()
            pass_heads(mask)
        first_step(at)
    lag = n_groups
    for key in range(len(items) + lag * (nb - 1)):
        for step in range(1, nb + 1):
            at = key - lag * (step - 1)
            if 0 <= at < len(items):
                later_step(at, step)

    for at, (mask, g) in enumerate(items):
        if mask:
            lo, width, order = groups[g]
            pltpu.make_async_remote_copy(
                src_ref=snd[g].at[mask, 0:own],
                dst_ref=out_ref.at[flip_all(ctx, mask), :, lo : lo + width],
                send_sem=out_ssem.at[at],
                recv_sem=out_rsem.at[at],
                device_id=peer(mask),
                device_id_type=MESH,
            ).wait_recv()
    for copy in sends:
        copy.wait_send()


def on_device(q_nope, q_rope, w_uk, w_uv, w_o, cache_kv, new_kv, block_order, cache_lengths):
    tok, heads, nope = q_nope.shape
    rope = q_rope.shape[2]
    latent, vdim = w_uk.shape[2], w_uv.shape[2]
    slots = cache_kv.shape[0]
    depth, width = w_o.shape
    n_ctx, n_head = lax.axis_size("ctx"), lax.axis_size("head")
    own = tok // n_head
    full = (
        own % 16 == 0
        and width % 256 == 0
        and slots % 128 == 0
        and tok % 128 == 0
        and n_ctx & (n_ctx - 1) == 0
        and n_head & (n_head - 1) == 0
        and n_head > 1
    )
    if not full:
        return plain_on_device(q_nope, q_rope, w_uk, w_uv, w_o, cache_kv, new_kv, block_order, cache_lengths)
    groups = tuple(column_groups(width, bits_of(n_head)))
    nb = len(bits_of(n_head))
    dims = (n_ctx, n_head, tok, heads, nope, rope, latent, vdim, slots, groups)
    bf16, f32 = jnp.bfloat16, jnp.float32
    n_items = n_ctx * len(groups)
    dma = pltpu.SemaphoreType.DMA
    vmem = pl.BlockSpec(memory_space=pltpu.VMEM)
    smem = pl.BlockSpec(memory_space=pltpu.SMEM)
    anywhere = pl.BlockSpec(memory_space=pl.ANY)
    scratch = [
        pltpu.VMEM((heads * tok, latent + rope), bf16),
        pltpu.VMEM((n_ctx, latent + rope, slots + tok), bf16),
        pltpu.VMEM((heads * tok, latent), f32),
        pltpu.VMEM((n_ctx, tok, heads * vdim), bf16),
        pltpu.VMEM(w_uv.shape, bf16),
        pltpu.VMEM(w_o.shape, bf16),
    ]
    scratch += [pltpu.VMEM((n_ctx, tok, g[1]), bf16) for g in groups] * 2
    scratch += [pltpu.VMEM((n_ctx, tok // 2, g[1]), f32) for g in groups]
    scratch += [
        dma((4,)),
        dma((n_ctx, 2)),
        dma((n_ctx, 2)),
        dma((n_ctx,)),
        dma((n_ctx,)),
        dma((n_items, nb)),
        dma((n_items, nb)),
        dma((n_items,)),
        dma((n_items,)),
    ]
    out = pl.pallas_call(
        functools.partial(kernel, dims),
        out_shape=jax.ShapeDtypeStruct((n_ctx, own, width), bf16),
        in_specs=[vmem, vmem, vmem, anywhere, anywhere, anywhere, anywhere, smem, smem],
        out_specs=vmem,
        scratch_shapes=scratch,
        compiler_params=pltpu.CompilerParams(
            collective_id=0, has_side_effects=True, vmem_limit_bytes=60 * 1024 * 1024
        ),
    )(
        q_nope.reshape(tok * heads, nope),
        q_rope.transpose(1, 2, 0),
        w_uk,
        w_uv,
        w_o,
        cache_kv.T,
        new_kv.T,
        block_order,
        cache_lengths,
    )
    return out.transpose(1, 0, 2).reshape(own, n_ctx * width)


def solution(mesh):
    in_specs = (
        P("ctx", "head", None),
        P("ctx", "head", None),
        P("head", None, None),
        P("head", None, None),
        P("head", "ctx"),
        P("ctx", None),
        P("ctx", None),
        P(),
        P(),
    )
    out_specs = P(("ctx", "head"), None)
    return jax.shard_map(
        on_device, mesh=mesh, in_specs=in_specs, out_specs=out_specs, check_vma=False
    )
```

```python
import functools

import jax
import jax.numpy as jnp
from jax import lax
from jax.experimental import pallas as pl
from jax.experimental.pallas import tpu as pltpu
from jax.sharding import PartitionSpec as P

neg_large = -1e30
MESH = pl.DeviceIdType.MESH


def plain_on_device(q_nope, q_rope, w_uk, w_uv, w_o, cache_kv, new_kv, block_order, cache_lengths):
    tok_rows, heads_here, nope_width = q_nope.shape
    latent_width = w_uk.shape[2]
    value_width = w_uv.shape[2]
    cache_rows = cache_kv.shape[0]
    shard_rows = cache_rows + tok_rows
    ctx_count = lax.axis_size("ctx")
    head_count = lax.axis_size("head")
    score_scale = float(nope_width + q_rope.shape[2]) ** (-0.5)
    query_rows = tok_rows * heads_here
    q_latent = jnp.einsum("thn,hnc->thc", q_nope, w_uk, preferred_element_type=jnp.float32)
    query = jnp.concatenate([q_latent, q_rope.astype(jnp.float32)], axis=2).astype(jnp.bfloat16)
    query = query.reshape(query_rows, query.shape[2])
    shard_ids = jnp.arange(ctx_count, dtype=jnp.int32)
    own_block = jnp.sum(jnp.where(shard_ids == lax.axis_index("ctx"), block_order, 0))
    query_pos = own_block * tok_rows + jnp.arange(query_rows, dtype=jnp.int32) // heads_here
    local_keys = jnp.concatenate([cache_kv, new_kv], axis=0)
    piece = lax.all_gather(local_keys, "ctx", axis=0, tiled=True)
    global_rows = jnp.arange(piece.shape[0], dtype=jnp.int32)
    owners = global_rows // shard_rows
    offsets = global_rows % shard_rows
    matches = owners[:, None] == shard_ids[None, :]
    lengths = jnp.sum(jnp.where(matches, cache_lengths[None, :], 0), axis=1)
    blocks = jnp.sum(jnp.where(matches, block_order[None, :], 0), axis=1)
    key_pos = blocks * tok_rows + offsets - cache_rows
    visible = jnp.where(
        (offsets < cache_rows)[None, :],
        (offsets < lengths)[None, :],
        key_pos[None, :] <= query_pos[:, None],
    )
    best = jnp.full((query_rows,), neg_large, jnp.float32)
    scores = (
        lax.dot_general(query, piece, (((1,), (1,)), ((), ())), preferred_element_type=jnp.float32)
        * score_scale
    )
    fresh = jnp.maximum(best, jnp.max(jnp.where(visible, scores, neg_large), axis=1))
    expo = jnp.where(visible, jnp.exp(scores - fresh[:, None]), 0.0)
    totals = jnp.sum(expo, axis=1)
    accum = jnp.dot(
        expo.astype(jnp.bfloat16), piece[:, :latent_width], preferred_element_type=jnp.float32
    )
    best, totals, accum = (fresh, totals, accum)
    latent_out = (
        (accum / totals[:, None]).astype(jnp.bfloat16).reshape(tok_rows, heads_here, latent_width)
    )
    head_out = jnp.einsum("thc,hcv->thv", latent_out, w_uv, preferred_element_type=jnp.float32)
    head_out = head_out.astype(jnp.bfloat16).reshape(tok_rows, heads_here * value_width)
    partial_rows = jnp.dot(
        lax.all_gather(head_out, "ctx", axis=0, tiled=True), w_o, preferred_element_type=jnp.float32
    )
    column_width = w_o.shape[1]
    own_rows = tok_rows // head_count
    grouped = partial_rows.reshape(ctx_count, head_count, own_rows, column_width)
    summed = lax.psum_scatter(grouped.astype(jnp.bfloat16), "head", scatter_dimension=1, tiled=True)
    regrouped = lax.all_to_all(summed, "ctx", split_axis=0, concat_axis=3, tiled=True)
    return regrouped.reshape(own_rows, ctx_count * column_width)


def flip(index, bit):
    return index + bit - 2 * bit * lax.rem(lax.div(index, bit), 2)


def flip_all(index, mask):
    bit = 1
    while bit <= mask:
        if mask & bit:
            index = flip(index, bit)
        bit *= 2
    return index


def bits_of(count):
    return [1 << k for k in range(count.bit_length() - 1)]


def low_bit(mask):
    return mask & -mask


def column_groups(width, head_bits):
    first = (width * 4 // 7) // 256 * 256
    near, far = head_bits[0], head_bits[1]
    return (
        (0, first // 2, near, tuple(b for b in head_bits if b != near)),
        (first, (width - first) // 2, far, tuple(b for b in head_bits if b != far)),
    )


def kernel(dims, qn_ref, qr_ref, uk_ref, uv_hbm, wo_hbm, ck_ref, nk_ref, order_ref, lens_ref, out_ref, *scratch):
    n_ctx, n_head, tok, heads, nope, rope, latent, vdim, slots, groups = dims
    n_groups = len(groups)
    query, kv, acc, ho, hx, uv_ref = scratch[:6]
    wide = scratch[6 : 6 + n_groups]
    snd = scratch[6 + n_groups : 6 + 2 * n_groups]
    rcv = scratch[6 + 2 * n_groups : 6 + 3 * n_groups]
    tot = scratch[6 + 3 * n_groups : 6 + 4 * n_groups]
    sems = scratch[6 + 4 * n_groups :]
    loc_sem, kv_ssem, kv_rsem, ho_ssem, ho_rsem, hx_ssem, hx_rsem, w_ssem, w_rsem = sems[:9]
    rs_ssem, rs_rsem, out_ssem, out_rsem = sems[9:]
    ctx, hd = lax.axis_index("ctx"), lax.axis_index("head")
    ctx_bits, head_bits = bits_of(n_ctx), bits_of(n_head)
    nb = len(head_bits)
    n_steps = nb - 1
    own = tok // n_head
    depth = heads * vdim
    keys = slots + tok
    rows = heads * tok
    f32, bf16 = jnp.float32, jnp.bfloat16

    def peer(ctx_mask=0, head_bit=0):
        return {
            "ctx": flip_all(ctx, ctx_mask),
            "head": flip(hd, head_bit) if head_bit else hd,
        }

    local = [
        pltpu.make_async_copy(ck_ref, kv.at[0, :, 0:slots], loc_sem.at[0]),
        pltpu.make_async_copy(nk_ref, kv.at[0, :, slots:keys], loc_sem.at[1]),
        pltpu.make_async_copy(uv_hbm, uv_ref, loc_sem.at[2]),
    ]

    def kept(g, swapped=False):
        lo, width, bit, _ = groups[g]
        upper = lax.rem(lax.div(hd, bit), 2)
        upper = 1 - upper if swapped else upper
        return pl.ds(pl.multiple_of(lo + width * upper, 128), width)

    for g in range(n_groups):
        local.append(
            pltpu.make_async_copy(wo_hbm.at[:, kept(g)], wide[g].at[0:depth], loc_sem.at[3 + g])
        )
    for copy in local:
        copy.start()

    barrier = pltpu.get_barrier_semaphore()
    for mask in range(1, n_ctx):
        pl.semaphore_signal(barrier, inc=1, device_id=peer(mask), device_id_type=MESH)
    swaps = [group[2] for group in groups]
    for bit in head_bits:
        for mask in range(n_ctx if bit in swaps else 1):
            pl.semaphore_signal(barrier, inc=1, device_id=peer(mask, bit), device_id_type=MESH)
    pl.semaphore_wait(barrier, n_ctx - 1 + nb + (n_ctx - 1) * len(swaps))

    sends = []

    def send(src, dst, ssem, rsem, device):
        copy = pltpu.make_async_remote_copy(
            src_ref=src, dst_ref=dst, send_sem=ssem, recv_sem=rsem, device_id=device, device_id_type=MESH
        )
        copy.start()
        sends.append(copy)
        return copy

    kv_in = {}
    spans = [(0, slots), (slots, keys)]

    def pass_keys(mask, part):
        lo, hi = spans[part]
        for bit in reversed(ctx_bits):
            if mask == 0 or bit < low_bit(mask):
                src = (ck_ref, nk_ref)[part] if mask == 0 else kv.at[mask, :, lo:hi]
                kv_in[mask | bit, part] = send(
                    src,
                    kv.at[mask | bit, :, lo:hi],
                    kv_ssem.at[mask | bit, part],
                    kv_rsem.at[mask | bit, part],
                    peer(bit),
                )

    for part in range(2):
        pass_keys(0, part)

    w_in = [
        send(
            wo_hbm.at[:, kept(g, True)],
            wide[g].at[depth : 2 * depth],
            w_ssem.at[g],
            w_rsem.at[g],
            peer(0, groups[g][2]),
        )
        for g in range(n_groups)
    ]

    order0 = tuple(head_bits)
    place = lax.broadcasted_iota(jnp.int32, (tok, 1), 0)
    block = place // own
    token = place % own
    for at, bit in enumerate(order0):
        digit = (block // (1 << (nb - 1 - at))) % 2
        mine = lax.rem(lax.div(hd, bit), 2)
        token = token + own * bit * (digit + mine - 2 * digit * mine)
    flat = lax.broadcasted_iota(jnp.int32, (tok, rows), 1)
    pick = (lax.broadcasted_iota(jnp.int32, (tok, tok), 1) == token).astype(bf16)
    q_all = qn_ref[...]
    for h in range(heads):
        choose = (flat == token * heads + h).astype(bf16)
        q_h = jnp.dot(choose, q_all, preferred_element_type=f32).astype(bf16)
        lat = jnp.dot(q_h, uk_ref[h], preferred_element_type=f32)
        span = slice(h * tok, (h + 1) * tok)
        query[span, 0:latent] = lat.astype(bf16)
        turned = lax.dot_general(pick, qr_ref[h], (((1,), (1,)), ((), ())), preferred_element_type=f32)
        query[span, latent : latent + rope] = turned.astype(bf16)

    scale = float(nope + rope) ** (-0.5)
    q_pos = order_ref[ctx] * tok + jnp.concatenate([token] * heads, axis=0)
    col = lax.broadcasted_iota(jnp.int32, (rows, keys), 1)

    best = total = None
    for mask in range(n_ctx):
        for part in range(2):
            if mask == 0:
                local[part].wait()
            else:
                kv_in[mask, part].wait_recv()
                pass_keys(mask, part)
        source = flip_all(ctx, mask)
        length = lens_ref[source]
        key_pos = col - slots + order_ref[source] * tok
        seen = jnp.where(col < slots, col - length + 1, key_pos - q_pos) <= 0
        s = jnp.dot(query[...], kv[mask], preferred_element_type=f32) * scale
        s = jnp.where(seen, s, neg_large)
        top = jnp.max(s, axis=1, keepdims=True)
        if mask:
            top = jnp.maximum(best, top)
        e = jnp.exp(s - top)
        part_sum = jnp.sum(e, axis=1, keepdims=True)
        mixed = lax.dot_general(
            e.astype(bf16), kv[mask, 0:latent, :], (((1,), (1,)), ((), ())), preferred_element_type=f32
        )
        if mask:
            shrink = jnp.exp(best - top)
            total = total * shrink + part_sum
            mixed = acc[...] * shrink + mixed
        else:
            total = part_sum
        best = top
        if mask < n_ctx - 1:
            acc[...] = mixed

    lat_out = (mixed / total).astype(bf16)
    local[2].wait()
    for h in range(heads):
        ho[0, :, h * vdim : (h + 1) * vdim] = jnp.dot(
            lat_out[h * tok : (h + 1) * tok], uv_ref[h], preferred_element_type=f32
        ).astype(bf16)
    ho_in, hx_in = {}, {}

    def pass_partner(g, mask, src):
        hx_in[g, mask] = send(
            src, hx.at[g, mask], hx_ssem.at[g, mask], hx_rsem.at[g, mask], peer(0, groups[g][2])
        )

    def pass_heads(mask):
        for bit in reversed(ctx_bits):
            if mask == 0 or bit < low_bit(mask):
                ho_in[mask | bit] = send(
                    ho.at[mask], ho.at[mask | bit], ho_ssem.at[mask | bit], ho_rsem.at[mask | bit], peer(bit)
                )
        if mask % 2 == 0:
            for g in range(n_groups):
                pass_partner(g, mask, ho.at[mask])

    def pass_across(g, mask):
        if mask % 2 == 0:
            hx_in[g, mask + 1] = send(
                hx.at[g, mask],
                hx.at[g, mask + 1],
                hx_ssem.at[g, mask + 1],
                hx_rsem.at[g, mask + 1],
                peer(1),
            )

    pass_heads(0)

    items = [(mask, g) for mask in range(n_ctx) for g in range(n_groups)]
    moving = {}

    def push(at, step):
        mask, g = items[at]
        size = tok >> (step + 1)
        moving[at, step] = send(
            snd[g].at[mask, size : 2 * size],
            rcv[g].at[mask, size : 2 * size],
            rs_ssem.at[at, step],
            rs_rsem.at[at, step],
            peer(0, groups[g][3][step]),
        )

    def at_block(p, order, other):
        m = sum(order[k] for k in range(nb) if p >> (nb - 1 - k) & 1) ^ other
        return sum(1 << (nb - 1 - k) for k in range(nb) if m & order0[k])

    def placed(x, order, other):
        spots = [at_block(p, order, other) for p in range(n_head)]
        return jnp.concatenate([x[k * own : (k + 1) * own] for k in spots], axis=0)

    def first_step(at):
        mask, g = items[at]
        lo, width, bit, steps = groups[g]
        order = steps + (bit,)
        x = jnp.concatenate([placed(ho[mask], order, 0), placed(hx[g, mask], order, bit)], axis=1)
        y = jnp.dot(x, wide[g][...], preferred_element_type=f32)
        tot[g][mask] = y[0 : tok // 2]
        snd[g][mask, tok // 2 : tok] = y[tok // 2 :].astype(bf16)
        push(at, 0)

    def later_step(at, step):
        mask, g = items[at]
        lo, width, bit, steps = groups[g]
        size = tok >> step
        moving[at, step - 1].wait_recv()
        y = tot[g][mask, 0:size] + rcv[g][mask, size : 2 * size].astype(f32)
        if step < n_steps:
            half = size // 2
            snd[g][mask, half:size] = y[half:].astype(bf16)
            tot[g][mask, 0:half] = y[:half]
            push(at, step)
            return
        snd[g][mask, 0:size] = y.astype(bf16)
        for side in range(2):
            if mask == 0 and side == 0:
                out_ref[ctx, :, kept(g)] = y[0:own].astype(bf16)
            else:
                send(
                    snd[g].at[mask, side * own : (side + 1) * own],
                    out_ref.at[ctx, :, kept(g)],
                    out_ssem.at[at, side],
                    out_rsem.at[at, side],
                    peer(mask, bit * side),
                )

    even = [mask for mask in range(2, n_ctx, 2)]
    for mask in sorted(even, key=lambda k: -low_bit(k)):
        ho_in[mask].wait_recv()
        pass_heads(mask)
    waited = set()
    for at, (mask, g) in enumerate(items):
        if mask % 2 and mask not in waited:
            waited.add(mask)
            ho_in[mask].wait_recv()
        hx_in[g, mask].wait_recv()
        pass_across(g, mask)
        if mask == 0:
            local[3 + g].wait()
            w_in[g].wait_recv()
        first_step(at)
    lag = n_groups
    for key in range(len(items) + lag * (n_steps - 1)):
        for step in range(1, n_steps + 1):
            at = key - lag * (step - 1)
            if 0 <= at < len(items):
                later_step(at, step)

    for at, (mask, g) in enumerate(items):
        lo, width, bit, steps = groups[g]
        for side in range(2):
            if mask or side:
                pltpu.make_async_remote_copy(
                    src_ref=snd[g].at[mask, side * own : (side + 1) * own],
                    dst_ref=out_ref.at[flip_all(ctx, mask), :, kept(g, side == 1)],
                    send_sem=out_ssem.at[at, side],
                    recv_sem=out_rsem.at[at, side],
                    device_id=peer(mask, bit * side),
                    device_id_type=MESH,
                ).wait_recv()
    for copy in sends:
        copy.wait_send()


def on_device(q_nope, q_rope, w_uk, w_uv, w_o, cache_kv, new_kv, block_order, cache_lengths):
    tok, heads, nope = q_nope.shape
    rope = q_rope.shape[2]
    latent, vdim = w_uk.shape[2], w_uv.shape[2]
    slots = cache_kv.shape[0]
    depth, width = w_o.shape
    n_ctx, n_head = lax.axis_size("ctx"), lax.axis_size("head")
    own = tok // n_head
    full = (
        own % 16 == 0
        and width % 256 == 0
        and slots % 128 == 0
        and tok % 128 == 0
        and n_ctx & (n_ctx - 1) == 0
        and n_head & (n_head - 1) == 0
        and n_ctx > 1
        and n_head > 3
        and width >= 512
    )
    if not full:
        return plain_on_device(q_nope, q_rope, w_uk, w_uv, w_o, cache_kv, new_kv, block_order, cache_lengths)
    groups = column_groups(width, bits_of(n_head))
    n_groups = len(groups)
    n_steps = len(bits_of(n_head)) - 1
    dims = (n_ctx, n_head, tok, heads, nope, rope, latent, vdim, slots, groups)
    bf16, f32 = jnp.bfloat16, jnp.float32
    n_items = n_ctx * n_groups
    dma = pltpu.SemaphoreType.DMA
    vmem = pl.BlockSpec(memory_space=pltpu.VMEM)
    smem = pl.BlockSpec(memory_space=pltpu.SMEM)
    anywhere = pl.BlockSpec(memory_space=pl.ANY)
    scratch = [
        pltpu.VMEM((heads * tok, latent + rope), bf16),
        pltpu.VMEM((n_ctx, latent + rope, slots + tok), bf16),
        pltpu.VMEM((heads * tok, latent), f32),
        pltpu.VMEM((n_ctx, tok, heads * vdim), bf16),
        pltpu.VMEM((n_groups, n_ctx, tok, heads * vdim), bf16),
        pltpu.VMEM(w_uv.shape, bf16),
    ]
    scratch += [pltpu.VMEM((2 * depth, g[1]), bf16) for g in groups]
    scratch += [pltpu.VMEM((n_ctx, tok, g[1]), bf16) for g in groups] * 2
    scratch += [pltpu.VMEM((n_ctx, tok // 2, g[1]), f32) for g in groups]
    scratch += [
        dma((3 + n_groups,)),
        dma((n_ctx, 2)),
        dma((n_ctx, 2)),
        dma((n_ctx,)),
        dma((n_ctx,)),
        dma((n_groups, n_ctx)),
        dma((n_groups, n_ctx)),
        dma((n_groups,)),
        dma((n_groups,)),
        dma((n_items, n_steps)),
        dma((n_items, n_steps)),
        dma((n_items, 2)),
        dma((n_items, 2)),
    ]
    out = pl.pallas_call(
        functools.partial(kernel, dims),
        out_shape=jax.ShapeDtypeStruct((n_ctx, own, width), bf16),
        in_specs=[vmem, vmem, vmem, anywhere, anywhere, anywhere, anywhere, smem, smem],
        out_specs=vmem,
        scratch_shapes=scratch,
        compiler_params=pltpu.CompilerParams(
            collective_id=0, has_side_effects=True, vmem_limit_bytes=60 * 1024 * 1024
        ),
    )(
        q_nope.reshape(tok * heads, nope),
        q_rope.transpose(1, 2, 0),
        w_uk,
        w_uv,
        w_o,
        cache_kv.T,
        new_kv.T,
        block_order,
        cache_lengths,
    )
    return out.transpose(1, 0, 2).reshape(own, n_ctx * width)


def solution(mesh):
    in_specs = (
        P("ctx", "head", None),
        P("ctx", "head", None),
        P("head", None, None),
        P("head", None, None),
        P("head", "ctx"),
        P("ctx", None),
        P("ctx", None),
        P(),
        P(),
    )
    out_specs = P(("ctx", "head"), None)
    return jax.shard_map(
        on_device, mesh=mesh, in_specs=in_specs, out_specs=out_specs, check_vma=False
    )
```

```python
import functools

import jax
import jax.numpy as jnp
from jax import lax
from jax.experimental import pallas as pl
from jax.experimental.pallas import tpu as pltpu
from jax.sharding import PartitionSpec as P

neg_large = -1e30
MESH = pl.DeviceIdType.MESH


def plain_on_device(q_nope, q_rope, w_uk, w_uv, w_o, cache_kv, new_kv, block_order, cache_lengths):
    tok_rows, heads_here, nope_width = q_nope.shape
    latent_width = w_uk.shape[2]
    value_width = w_uv.shape[2]
    cache_rows = cache_kv.shape[0]
    shard_rows = cache_rows + tok_rows
    ctx_count = lax.axis_size("ctx")
    head_count = lax.axis_size("head")
    score_scale = float(nope_width + q_rope.shape[2]) ** (-0.5)
    query_rows = tok_rows * heads_here
    q_latent = jnp.einsum("thn,hnc->thc", q_nope, w_uk, preferred_element_type=jnp.float32)
    query = jnp.concatenate([q_latent, q_rope.astype(jnp.float32)], axis=2).astype(jnp.bfloat16)
    query = query.reshape(query_rows, query.shape[2])
    shard_ids = jnp.arange(ctx_count, dtype=jnp.int32)
    own_block = jnp.sum(jnp.where(shard_ids == lax.axis_index("ctx"), block_order, 0))
    query_pos = own_block * tok_rows + jnp.arange(query_rows, dtype=jnp.int32) // heads_here
    local_keys = jnp.concatenate([cache_kv, new_kv], axis=0)
    piece = lax.all_gather(local_keys, "ctx", axis=0, tiled=True)
    global_rows = jnp.arange(piece.shape[0], dtype=jnp.int32)
    owners = global_rows // shard_rows
    offsets = global_rows % shard_rows
    matches = owners[:, None] == shard_ids[None, :]
    lengths = jnp.sum(jnp.where(matches, cache_lengths[None, :], 0), axis=1)
    blocks = jnp.sum(jnp.where(matches, block_order[None, :], 0), axis=1)
    key_pos = blocks * tok_rows + offsets - cache_rows
    visible = jnp.where(
        (offsets < cache_rows)[None, :],
        (offsets < lengths)[None, :],
        key_pos[None, :] <= query_pos[:, None],
    )
    best = jnp.full((query_rows,), neg_large, jnp.float32)
    scores = (
        lax.dot_general(query, piece, (((1,), (1,)), ((), ())), preferred_element_type=jnp.float32)
        * score_scale
    )
    fresh = jnp.maximum(best, jnp.max(jnp.where(visible, scores, neg_large), axis=1))
    expo = jnp.where(visible, jnp.exp(scores - fresh[:, None]), 0.0)
    totals = jnp.sum(expo, axis=1)
    accum = jnp.dot(
        expo.astype(jnp.bfloat16), piece[:, :latent_width], preferred_element_type=jnp.float32
    )
    best, totals, accum = (fresh, totals, accum)
    latent_out = (
        (accum / totals[:, None]).astype(jnp.bfloat16).reshape(tok_rows, heads_here, latent_width)
    )
    head_out = jnp.einsum("thc,hcv->thv", latent_out, w_uv, preferred_element_type=jnp.float32)
    head_out = head_out.astype(jnp.bfloat16).reshape(tok_rows, heads_here * value_width)
    partial_rows = jnp.dot(
        lax.all_gather(head_out, "ctx", axis=0, tiled=True), w_o, preferred_element_type=jnp.float32
    )
    column_width = w_o.shape[1]
    own_rows = tok_rows // head_count
    grouped = partial_rows.reshape(ctx_count, head_count, own_rows, column_width)
    summed = lax.psum_scatter(grouped.astype(jnp.bfloat16), "head", scatter_dimension=1, tiled=True)
    regrouped = lax.all_to_all(summed, "ctx", split_axis=0, concat_axis=3, tiled=True)
    return regrouped.reshape(own_rows, ctx_count * column_width)


def flip(index, bit):
    return index + bit - 2 * bit * lax.rem(lax.div(index, bit), 2)


def flip_all(index, mask):
    bit = 1
    while bit <= mask:
        if mask & bit:
            index = flip(index, bit)
        bit *= 2
    return index


def bits_of(count):
    return [1 << k for k in range(count.bit_length() - 1)]


def low_bit(mask):
    return mask & -mask


def column_groups(width, head_bits):
    first = (width * 3 // 7) // 256 * 256
    near, far = head_bits[0], head_bits[1]
    return (
        (0, first // 2, near, tuple(b for b in head_bits if b != near)),
        (first, (width - first) // 2, far, tuple(b for b in head_bits if b != far)),
    )


def kernel(dims, qn_ref, qr_ref, uk_ref, uv_hbm, wo_hbm, ck_ref, nk_ref, order_ref, lens_ref, out_ref, *scratch):
    n_ctx, n_head, tok, heads, nope, rope, latent, vdim, slots, groups = dims
    n_groups = len(groups)
    query, kv, acc, ho, hx, uv_ref = scratch[:6]
    wide = scratch[6 : 6 + n_groups]
    snd = scratch[6 + n_groups : 6 + 2 * n_groups]
    rcv = scratch[6 + 2 * n_groups : 6 + 3 * n_groups]
    tot = scratch[6 + 3 * n_groups : 6 + 4 * n_groups]
    sems = scratch[6 + 4 * n_groups :]
    loc_sem, kv_ssem, kv_rsem, ho_ssem, ho_rsem, hx_ssem, hx_rsem, w_ssem, w_rsem = sems[:9]
    rs_ssem, rs_rsem, out_ssem, out_rsem = sems[9:]
    ctx, hd = lax.axis_index("ctx"), lax.axis_index("head")
    ctx_bits, head_bits = bits_of(n_ctx), bits_of(n_head)
    nb = len(head_bits)
    n_steps = nb - 1
    own = tok // n_head
    depth = heads * vdim
    keys = slots + tok
    rows = heads * tok
    f32, bf16 = jnp.float32, jnp.bfloat16

    def peer(ctx_mask=0, head_bit=0):
        return {
            "ctx": flip_all(ctx, ctx_mask),
            "head": flip(hd, head_bit) if head_bit else hd,
        }

    local = [
        pltpu.make_async_copy(ck_ref, kv.at[0, :, 0:slots], loc_sem.at[0]),
        pltpu.make_async_copy(nk_ref, kv.at[0, :, slots:keys], loc_sem.at[1]),
        pltpu.make_async_copy(uv_hbm, uv_ref, loc_sem.at[2]),
    ]

    def kept(g, swapped=False):
        lo, width, bit, _ = groups[g]
        upper = lax.rem(lax.div(hd, bit), 2)
        upper = 1 - upper if swapped else upper
        return pl.ds(pl.multiple_of(lo + width * upper, 128), width)

    for g in range(n_groups):
        local.append(
            pltpu.make_async_copy(wo_hbm.at[:, kept(g)], wide[g].at[0:depth], loc_sem.at[3 + g])
        )
    for copy in local:
        copy.start()

    barrier = pltpu.get_barrier_semaphore()
    for mask in range(1, n_ctx):
        pl.semaphore_signal(barrier, inc=1, device_id=peer(mask), device_id_type=MESH)
    swaps = [group[2] for group in groups]
    for bit in head_bits:
        for mask in range(n_ctx if bit in swaps else 1):
            pl.semaphore_signal(barrier, inc=1, device_id=peer(mask, bit), device_id_type=MESH)
    pl.semaphore_wait(barrier, n_ctx - 1 + nb + (n_ctx - 1) * len(swaps))

    sends = []

    def send(src, dst, ssem, rsem, device):
        copy = pltpu.make_async_remote_copy(
            src_ref=src, dst_ref=dst, send_sem=ssem, recv_sem=rsem, device_id=device, device_id_type=MESH
        )
        copy.start()
        sends.append(copy)
        return copy

    kv_in = {}
    spans = [(0, slots), (slots, keys)]

    def pass_keys(mask, part):
        lo, hi = spans[part]
        for bit in reversed(ctx_bits):
            if mask == 0 or bit < low_bit(mask):
                src = (ck_ref, nk_ref)[part] if mask == 0 else kv.at[mask, :, lo:hi]
                kv_in[mask | bit, part] = send(
                    src,
                    kv.at[mask | bit, :, lo:hi],
                    kv_ssem.at[mask | bit, part],
                    kv_rsem.at[mask | bit, part],
                    peer(bit),
                )

    for part in range(2):
        pass_keys(0, part)

    w_in = [
        send(
            wo_hbm.at[:, kept(g, True)],
            wide[g].at[depth : 2 * depth],
            w_ssem.at[g],
            w_rsem.at[g],
            peer(0, groups[g][2]),
        )
        for g in range(n_groups)
    ]

    order0 = tuple(head_bits)
    place = lax.broadcasted_iota(jnp.int32, (tok, 1), 0)
    block = place // own
    token = place % own
    for at, bit in enumerate(order0):
        digit = (block // (1 << (nb - 1 - at))) % 2
        mine = lax.rem(lax.div(hd, bit), 2)
        token = token + own * bit * (digit + mine - 2 * digit * mine)
    flat = lax.broadcasted_iota(jnp.int32, (tok, rows), 1)
    pick = (lax.broadcasted_iota(jnp.int32, (tok, tok), 1) == token).astype(bf16)
    q_all = qn_ref[...]
    for h in range(heads):
        choose = (flat == token * heads + h).astype(bf16)
        q_h = jnp.dot(choose, q_all, preferred_element_type=f32).astype(bf16)
        lat = jnp.dot(q_h, uk_ref[h], preferred_element_type=f32)
        span = slice(h * tok, (h + 1) * tok)
        query[span, 0:latent] = lat.astype(bf16)
        turned = lax.dot_general(pick, qr_ref[h], (((1,), (1,)), ((), ())), preferred_element_type=f32)
        query[span, latent : latent + rope] = turned.astype(bf16)

    scale = float(nope + rope) ** (-0.5)
    q_pos = order_ref[ctx] * tok + jnp.concatenate([token] * heads, axis=0)
    col = lax.broadcasted_iota(jnp.int32, (rows, keys), 1)

    best = total = None
    for mask in range(n_ctx):
        for part in range(2):
            if mask == 0:
                local[part].wait()
            else:
                kv_in[mask, part].wait_recv()
                pass_keys(mask, part)
        source = flip_all(ctx, mask)
        length = lens_ref[source]
        key_pos = col - slots + order_ref[source] * tok
        seen = jnp.where(col < slots, col - length + 1, key_pos - q_pos) <= 0
        s = jnp.dot(query[...], kv[mask], preferred_element_type=f32) * scale
        s = jnp.where(seen, s, neg_large)
        top = jnp.max(s, axis=1, keepdims=True)
        if mask:
            top = jnp.maximum(best, top)
        e = jnp.exp(s - top)
        part_sum = jnp.sum(e, axis=1, keepdims=True)
        mixed = lax.dot_general(
            e.astype(bf16), kv[mask, 0:latent, :], (((1,), (1,)), ((), ())), preferred_element_type=f32
        )
        if mask:
            shrink = jnp.exp(best - top)
            total = total * shrink + part_sum
            mixed = acc[...] * shrink + mixed
        else:
            total = part_sum
        best = top
        if mask < n_ctx - 1:
            acc[...] = mixed

    lat_out = (mixed / total).astype(bf16)
    local[2].wait()
    for h in range(heads):
        ho[0, :, h * vdim : (h + 1) * vdim] = jnp.dot(
            lat_out[h * tok : (h + 1) * tok], uv_ref[h], preferred_element_type=f32
        ).astype(bf16)
    ho_in, hx_in = {}, {}

    def pass_partner(g, mask, src):
        hx_in[g, mask] = send(
            src, hx.at[g, mask], hx_ssem.at[g, mask], hx_rsem.at[g, mask], peer(0, groups[g][2])
        )

    def pass_heads(mask):
        for bit in reversed(ctx_bits):
            if mask == 0 or bit < low_bit(mask):
                ho_in[mask | bit] = send(
                    ho.at[mask], ho.at[mask | bit], ho_ssem.at[mask | bit], ho_rsem.at[mask | bit], peer(bit)
                )
        if mask % 2 == 0:
            for g in range(n_groups):
                pass_partner(g, mask, ho.at[mask])

    def pass_across(g, mask):
        if mask % 2 == 0:
            hx_in[g, mask + 1] = send(
                hx.at[g, mask],
                hx.at[g, mask + 1],
                hx_ssem.at[g, mask + 1],
                hx_rsem.at[g, mask + 1],
                peer(1),
            )

    pass_heads(0)

    items = [(mask, g) for mask in range(n_ctx) for g in range(n_groups)]
    moving = {}

    def push(at, step):
        mask, g = items[at]
        size = tok >> (step + 1)
        moving[at, step] = send(
            snd[g].at[mask, size : 2 * size],
            rcv[g].at[mask, size : 2 * size],
            rs_ssem.at[at, step],
            rs_rsem.at[at, step],
            peer(0, groups[g][3][step]),
        )

    def at_block(p, order, other):
        m = sum(order[k] for k in range(nb) if p >> (nb - 1 - k) & 1) ^ other
        return sum(1 << (nb - 1 - k) for k in range(nb) if m & order0[k])

    def placed(x, order, other):
        spots = [at_block(p, order, other) for p in range(n_head)]
        return jnp.concatenate([x[k * own : (k + 1) * own] for k in spots], axis=0)

    def first_step(at):
        mask, g = items[at]
        lo, width, bit, steps = groups[g]
        order = steps + (bit,)
        x = jnp.concatenate([placed(ho[mask], order, 0), placed(hx[g, mask], order, bit)], axis=1)
        y = jnp.dot(x, wide[g][...], preferred_element_type=f32)
        tot[g][mask] = y[0 : tok // 2]
        snd[g][mask, tok // 2 : tok] = y[tok // 2 :].astype(bf16)
        push(at, 0)

    def later_step(at, step):
        mask, g = items[at]
        lo, width, bit, steps = groups[g]
        size = tok >> step
        moving[at, step - 1].wait_recv()
        y = tot[g][mask, 0:size] + rcv[g][mask, size : 2 * size].astype(f32)
        if step < n_steps:
            half = size // 2
            snd[g][mask, half:size] = y[half:].astype(bf16)
            tot[g][mask, 0:half] = y[:half]
            push(at, step)
            return
        snd[g][mask, 0:size] = y.astype(bf16)
        for side in range(2):
            if mask == 0 and side == 0:
                out_ref[ctx, :, kept(g)] = y[0:own].astype(bf16)
            else:
                send(
                    snd[g].at[mask, side * own : (side + 1) * own],
                    out_ref.at[ctx, :, kept(g)],
                    out_ssem.at[at, side],
                    out_rsem.at[at, side],
                    peer(mask, bit * side),
                )

    even = [mask for mask in range(2, n_ctx, 2)]
    for mask in sorted(even, key=lambda k: -low_bit(k)):
        ho_in[mask].wait_recv()
        pass_heads(mask)
    waited = set()

    def begin(at):
        mask, g = items[at]
        if mask % 2 and mask not in waited:
            waited.add(mask)
            ho_in[mask].wait_recv()
        hx_in[g, mask].wait_recv()
        pass_across(g, mask)
        if mask == 0:
            local[3 + g].wait()
            w_in[g].wait_recv()
        first_step(at)

    lag = 3
    for key in range(len(items) + lag * n_steps):
        for step in range(n_steps + 1):
            at = key - lag * step
            if 0 <= at < len(items):
                if step:
                    later_step(at, step)
                else:
                    begin(at)

    for at, (mask, g) in enumerate(items):
        lo, width, bit, steps = groups[g]
        for side in range(2):
            if mask or side:
                pltpu.make_async_remote_copy(
                    src_ref=snd[g].at[mask, side * own : (side + 1) * own],
                    dst_ref=out_ref.at[flip_all(ctx, mask), :, kept(g, side == 1)],
                    send_sem=out_ssem.at[at, side],
                    recv_sem=out_rsem.at[at, side],
                    device_id=peer(mask, bit * side),
                    device_id_type=MESH,
                ).wait_recv()
    for copy in sends:
        copy.wait_send()


def on_device(q_nope, q_rope, w_uk, w_uv, w_o, cache_kv, new_kv, block_order, cache_lengths):
    tok, heads, nope = q_nope.shape
    rope = q_rope.shape[2]
    latent, vdim = w_uk.shape[2], w_uv.shape[2]
    slots = cache_kv.shape[0]
    depth, width = w_o.shape
    n_ctx, n_head = lax.axis_size("ctx"), lax.axis_size("head")
    own = tok // n_head
    full = (
        own % 16 == 0
        and width % 256 == 0
        and slots % 128 == 0
        and tok % 128 == 0
        and n_ctx & (n_ctx - 1) == 0
        and n_head & (n_head - 1) == 0
        and n_ctx > 1
        and n_head > 3
        and width >= 512
    )
    if not full:
        return plain_on_device(q_nope, q_rope, w_uk, w_uv, w_o, cache_kv, new_kv, block_order, cache_lengths)
    groups = column_groups(width, bits_of(n_head))
    n_groups = len(groups)
    n_steps = len(bits_of(n_head)) - 1
    dims = (n_ctx, n_head, tok, heads, nope, rope, latent, vdim, slots, groups)
    bf16, f32 = jnp.bfloat16, jnp.float32
    n_items = n_ctx * n_groups
    dma = pltpu.SemaphoreType.DMA
    vmem = pl.BlockSpec(memory_space=pltpu.VMEM)
    smem = pl.BlockSpec(memory_space=pltpu.SMEM)
    anywhere = pl.BlockSpec(memory_space=pl.ANY)
    scratch = [
        pltpu.VMEM((heads * tok, latent + rope), bf16),
        pltpu.VMEM((n_ctx, latent + rope, slots + tok), bf16),
        pltpu.VMEM((heads * tok, latent), f32),
        pltpu.VMEM((n_ctx, tok, heads * vdim), bf16),
        pltpu.VMEM((n_groups, n_ctx, tok, heads * vdim), bf16),
        pltpu.VMEM(w_uv.shape, bf16),
    ]
    scratch += [pltpu.VMEM((2 * depth, g[1]), bf16) for g in groups]
    scratch += [pltpu.VMEM((n_ctx, tok, g[1]), bf16) for g in groups] * 2
    scratch += [pltpu.VMEM((n_ctx, tok // 2, g[1]), f32) for g in groups]
    scratch += [
        dma((3 + n_groups,)),
        dma((n_ctx, 2)),
        dma((n_ctx, 2)),
        dma((n_ctx,)),
        dma((n_ctx,)),
        dma((n_groups, n_ctx)),
        dma((n_groups, n_ctx)),
        dma((n_groups,)),
        dma((n_groups,)),
        dma((n_items, n_steps)),
        dma((n_items, n_steps)),
        dma((n_items, 2)),
        dma((n_items, 2)),
    ]
    out = pl.pallas_call(
        functools.partial(kernel, dims),
        out_shape=jax.ShapeDtypeStruct((n_ctx, own, width), bf16),
        in_specs=[vmem, vmem, vmem, anywhere, anywhere, anywhere, anywhere, smem, smem],
        out_specs=vmem,
        scratch_shapes=scratch,
        compiler_params=pltpu.CompilerParams(
            collective_id=0, has_side_effects=True, vmem_limit_bytes=60 * 1024 * 1024
        ),
    )(
        q_nope.reshape(tok * heads, nope),
        q_rope.transpose(1, 2, 0),
        w_uk,
        w_uv,
        w_o,
        cache_kv.T,
        new_kv.T,
        block_order,
        cache_lengths,
    )
    return out.transpose(1, 0, 2).reshape(own, n_ctx * width)


def solution(mesh):
    in_specs = (
        P("ctx", "head", None),
        P("ctx", "head", None),
        P("head", None, None),
        P("head", None, None),
        P("head", "ctx"),
        P("ctx", None),
        P("ctx", None),
        P(),
        P(),
    )
    out_specs = P(("ctx", "head"), None)
    return jax.shard_map(
        on_device, mesh=mesh, in_specs=in_specs, out_specs=out_specs, check_vma=False
    )
```
